32 devices in a mesh: grp: 2 (over y), ct: 4 (over z), tm: 2 (over x), pol: 2 (over core).
Axes of the slice: x: 2, y: 2, z: 4, core: 2. Of those that a mesh axis runs over, the one named last changes fastest.
Arguments:
- voltages: bfloat16 [2048, 98304], P(('grp', 'ct', 'pol'), 'tm'), parts along dimension 0, may hold values from -4 to 4
- pfb_coeffs: float32 [4, 16384], replicated, may hold values from -3 to 3
- beam_delays: float32 [4, 1024], replicated, may hold values from -512 to 512
- slot_of_input: int32 [1024], replicated, may hold values from 0 to 1023, each once
- block_list: int32 [2, 2], replicated, may hold values from 0 to 15, as said below
Outputs:
- visibilities: bfloat16 [64, 4, 2, 64, 8192], P('tm', 'grp', None, None, ('ct', 'pol')), parts along dimension 1
- beams: bfloat16 [8, 6, 2, 8192], P('grp', 'tm', None, ('ct', 'pol')), parts along dimension 0
The draws below stay inside these ranges and needn't reach their ends.
There are 2 independent parts, one for each index of `grp`. The reference program is written for one: setup_inputs(seed, part) draws one part's arguments, and reference() takes and returns one part's arrays. A program takes and returns all parts, laid end to end along the dimension named above; an argument that names none is the same for every part. Nothing has to cross between parts.
Inputs may be any that keep to these rules, and one draw needn't show every extreme that they name: slot_of_input holds every number below 1024 once. `block_list`: each pair is a block row and a block column of 64-input groups with the row at least the column; the first pair lies in the last block row and the last pair in the first block column.
All inputs are finite; a program needn't handle non-finite values.
Results may differ from the reference program's by a relative error of at most 0.011.
Values may be sent and summed in bfloat16 or wider, within the bound.
A program may use at most 320 MiB of HBM per device.

```python
import math
import jax
import jax.numpy as jnp
from jax import lax

NIN = 1024
NCH = 8192
BLK = 64
TAPS = 4
FFT_A = 128
S_DEV = 3
NBLK = 2
NBEAM = 4
FRAME = 16384
FFT_B = 128
SPECTRA = 6
N_TM = 2


def draw_block_list(key, part):
    key = jax.random.fold_in(key, 7)
    groups = NIN // BLK
    first_pick = jax.random.randint(jax.random.fold_in(key, 101), (NBLK,), 0, groups, dtype=jnp.int32)
    second_pick = jax.random.randint(jax.random.fold_in(key, 202), (NBLK,), 0, groups, dtype=jnp.int32)
    rows_pick = jnp.maximum(first_pick, second_pick)
    cols_pick = jnp.minimum(first_pick, second_pick)
    rows_pick = rows_pick.at[0].set(groups - 1)
    cols_pick = cols_pick.at[NBLK - 1].set(0)
    return jnp.stack([rows_pick, cols_pick], axis=1).astype(jnp.int32)


def shard_levels(rng, shape, shards, smallest, largest):
    factor_of, own = 1.0, jax.random.fold_in(rng, 6)
    for axis_at, parts in shards:
        heights = jnp.exp(jax.random.uniform(jax.random.fold_in(own, axis_at), (parts,), jnp.float32, smallest / len(shards), largest / len(shards)))
        factor_of = factor_of * jnp.repeat(heights, shape[axis_at] // parts).reshape([-1 if axis == axis_at else 1 for axis in range(len(shape))])
    return factor_of


def gaussian(own_key, dims, scale, limit, cuts=(), kind=jnp.bfloat16):
    values = scale * jax.random.normal(own_key, dims, jnp.float32)
    if cuts:
        values = values * shard_levels(own_key, dims, cuts, -0.22, 0.18)
    return jnp.clip(values, -limit, limit).astype(kind)


def setup_inputs(seed: int = 0, part: int = 0) -> dict:
    key_list = jax.random.split(jax.random.key(seed), 6)
    part_splits = jax.random.split(jax.random.fold_in(key_list[5], part), 6)
    return {
        "voltages": gaussian(part_splits[0], (NIN, SPECTRA * FRAME), 0.5, 4.0, ((0, 8), (1, 2))),
        "pfb_coeffs": gaussian(key_list[1], (TAPS, FRAME), 0.5, 3.0, (), jnp.float32),
        "beam_delays": jnp.clip(jax.random.uniform(key_list[2], (NBEAM, NIN), jnp.float32, -512.0, 512.0), -512.0, 512.0),
        "slot_of_input": jax.random.permutation(key_list[3], NIN).astype(jnp.int32),
        "block_list": draw_block_list(jax.random.fold_in(key_list[5], 71), part),
    }


def make_tables(first_len, second_len):
    frame_len = first_len * second_len
    half_len = second_len // 2
    rows_a = jnp.arange(first_len, dtype=jnp.int32)
    phase_a = ((rows_a[:, None] * rows_a[None, :]) % first_len).astype(jnp.float32) * (2.0 * math.pi / first_len)
    first_table = (jnp.stack([jnp.cos(phase_a), -jnp.sin(phase_a)]) * (first_len ** -0.5)).astype(jnp.bfloat16)
    cols_b = jnp.arange(second_len, dtype=jnp.int32)
    phase_t = ((rows_a[:, None] * cols_b[None, :]) % frame_len).astype(jnp.float32) * (2.0 * math.pi / frame_len)
    twist_re = jnp.cos(phase_t)
    twist_im = -jnp.sin(phase_t)
    rows_h = jnp.arange(half_len, dtype=jnp.int32)
    phase_b = ((rows_h[:, None] * cols_b[None, :]) % second_len).astype(jnp.float32) * (2.0 * math.pi / second_len)
    cos_b = jnp.cos(phase_b) * (second_len ** -0.5)
    sin_b = -jnp.sin(phase_b) * (second_len ** -0.5)
    second = jnp.stack([jnp.stack([cos_b, -sin_b]), jnp.stack([sin_b, cos_b])]).astype(jnp.bfloat16)
    return first_table, twist_re, twist_im, second


def settle(values):
    return lax.optimization_barrier(values.astype(jnp.bfloat16)).astype(jnp.float32)


def reference(voltages, pfb_coeffs, beam_delays, slot_of_input, block_list):
    first_table, twist_re, twist_im, second = make_tables(FFT_A, FFT_B)
    groups = NIN // BLK
    frames = voltages.reshape(groups, BLK, SPECTRA, FRAME)

    def channelize(group_frames):
        leading = jnp.zeros((BLK, TAPS - 1, FRAME), group_frames.dtype)
        extended = jnp.concatenate([leading, group_frames], axis=1)
        filtered = jnp.zeros((BLK, SPECTRA, FRAME), jnp.float32)
        for tap_index in range(TAPS):
            filtered = filtered + pfb_coeffs[tap_index][None, None, :] * extended[:, tap_index:tap_index + SPECTRA].astype(jnp.float32)
        shaped = filtered.astype(jnp.bfloat16).reshape(BLK, SPECTRA, FFT_A, FFT_B)
        section_one = jnp.einsum('ckn,rsnm->rsckm', first_table.astype(jnp.float32), shaped.astype(jnp.float32))
        real_part = section_one[:, :, 0] * twist_re - section_one[:, :, 1] * twist_im
        imag_part = section_one[:, :, 0] * twist_im + section_one[:, :, 1] * twist_re
        twisted = jnp.stack([real_part, imag_part], 2).astype(jnp.bfloat16)
        result = jnp.einsum('ocqm,rsckm->rsoqk', second.astype(jnp.float32), twisted.astype(jnp.float32))
        return result.astype(jnp.bfloat16).reshape(BLK, SPECTRA, 2, NCH)

    spectra = lax.map(channelize, frames).reshape(NIN, SPECTRA, 2, NCH)
    channel_count = math.gcd(NCH, 512)
    norm_scale = NIN ** -0.5

    def per_block(block_index):
        first_channel = block_index * channel_count
        channel_slab = lax.dynamic_slice_in_dim(spectra, first_channel, channel_count, 3)
        logical = jnp.take(channel_slab, slot_of_input, axis=0).astype(jnp.float32)
        channels = (first_channel + jnp.arange(channel_count, dtype=jnp.int32)).astype(jnp.float32)
        ratio = NCH / (NCH + channels)
        phases = (beam_delays[:, :, None] * ratio[None, None, :]) * (2.0 * math.pi)
        weight_re = settle(jnp.cos(phases) * norm_scale)
        weight_im = settle(-jnp.sin(phases) * norm_scale)
        weights = jnp.stack([jnp.stack([weight_re, -weight_im], 1), jnp.stack([weight_im, weight_re], 1)], 1)
        beam_part = jnp.einsum('eozlk,lszk->esok', weights, logical)
        outputs = []
        for pair_index in range(NBLK):
            left_rows = lax.dynamic_slice_in_dim(logical, block_list[pair_index, 0] * BLK, BLK, 0)
            right_rows = lax.dynamic_slice_in_dim(logical, block_list[pair_index, 1] * BLK, BLK, 0)
            swapped = jnp.stack([-right_rows[:, :, 1], right_rows[:, :, 0]], 2)
            paired = jnp.stack([right_rows, swapped], 0).reshape(2, BLK, N_TM, S_DEV, 2, channel_count)
            left_rows = left_rows.reshape(BLK, N_TM, S_DEV, 2, channel_count)
            partial_value = settle(jnp.einsum('iuszk,ojuszk->uiojk', left_rows, paired))
            outputs.append(jnp.sum(partial_value, axis=0))
        return beam_part, jnp.stack(outputs, 1)

    beam_stack, vis_stack = lax.map(per_block, jnp.arange(NCH // channel_count, dtype=jnp.int32))
    beams = jnp.moveaxis(beam_stack, 0, 3).reshape(NBEAM, SPECTRA, 2, NCH).astype(jnp.bfloat16)
    visibilities = jnp.moveaxis(vis_stack, 0, 4).reshape(BLK, NBLK, 2, BLK, NCH).astype(jnp.bfloat16)
    return visibilities, beams
```

```python
import math

import jax
import jax.numpy as jnp
from jax import lax
from jax.experimental import pallas as pl
from jax.experimental.pallas import tpu as pltpu
from jax.sharding import PartitionSpec as P

NCH = 8192
BLK = 64
FFT_A = 128
FFT_B = 128


def shifted(block, axis, distance):
    devices = range(lax.axis_size(axis))
    route = [(i - distance, i) for i in devices if i - distance in devices]
    return lax.ppermute(block, axis, route)


def make_tables(first_len, second_len):
    frame_len = first_len * second_len
    half_len = second_len // 2
    rows_a = jnp.arange(first_len, dtype=jnp.int32)
    phase_a = (rows_a[:, None] * rows_a[None, :] % first_len).astype(jnp.float32) * (
        2.0 * math.pi / first_len
    )
    first_table = (jnp.stack([jnp.cos(phase_a), -jnp.sin(phase_a)]) * first_len ** (-0.5)).astype(
        jnp.bfloat16
    )
    cols_b = jnp.arange(second_len, dtype=jnp.int32)
    phase_t = (rows_a[:, None] * cols_b[None, :] % frame_len).astype(jnp.float32) * (
        2.0 * math.pi / frame_len
    )
    twist_re = jnp.cos(phase_t)
    twist_im = -jnp.sin(phase_t)
    rows_h = jnp.arange(half_len, dtype=jnp.int32)
    phase_b = (rows_h[:, None] * cols_b[None, :] % second_len).astype(jnp.float32) * (
        2.0 * math.pi / second_len
    )
    cos_b = jnp.cos(phase_b) * second_len ** (-0.5)
    sin_b = -jnp.sin(phase_b) * second_len ** (-0.5)
    second = jnp.stack([jnp.stack([cos_b, -sin_b]), jnp.stack([sin_b, cos_b])]).astype(jnp.bfloat16)
    return (first_table, twist_re, twist_im, second)


def beam_kernel(weight_re_ref, weight_im_ref, spectra_ref, out_ref):
    beam_count, shards, rows, lanes = weight_re_ref.shape
    step = 16
    for lane in range(0, lanes, 128):
        cols = pl.ds(lane, 128)

        def add(t, totals):
            d = t // (rows // step)
            at = pl.ds(pl.multiple_of(t % (rows // step) * step, step), step)
            re = spectra_ref[d, 0, at, cols].astype(jnp.float32)
            im = spectra_ref[d, 1, at, cols].astype(jnp.float32)
            sums = []
            for e in range(beam_count):
                w_re = weight_re_ref[e, d, at, cols].astype(jnp.float32)
                w_im = weight_im_ref[e, d, at, cols].astype(jnp.float32)
                sums.append(totals[2 * e] + (w_re * re - w_im * im))
                sums.append(totals[2 * e + 1] + (w_im * re + w_re * im))
            return tuple(sums)

        zeros = tuple(jnp.zeros((step, 128), jnp.float32) for _ in range(2 * beam_count))
        totals = lax.fori_loop(0, shards * rows // step, add, zeros)
        out_ref[:, cols] = jnp.concatenate(
            [jnp.sum(total, axis=0, keepdims=True) for total in totals], axis=0
        )


def form_beams(weight_re, weight_im, spectra):
    beam_count, shards, rows, channel_count = weight_re.shape
    block = min(256, channel_count)
    weight_spec = pl.BlockSpec((beam_count, shards, rows, block), lambda k: (0, 0, 0, k))
    return pl.pallas_call(
        beam_kernel,
        grid=(channel_count // block,),
        in_specs=[
            weight_spec,
            weight_spec,
            pl.BlockSpec((shards, 2, rows, block), lambda k: (0, 0, 0, k)),
        ],
        out_specs=pl.BlockSpec((2 * beam_count, block), lambda k: (0, k)),
        out_shape=jax.ShapeDtypeStruct((2 * beam_count, channel_count), jnp.float32),
        compiler_params=pltpu.CompilerParams(vmem_limit_bytes=40 * 2**20),
        cost_estimate=pl.CostEstimate(
            flops=16 * beam_count * shards * rows * channel_count,
            bytes_accessed=4 * (beam_count + 1) * shards * rows * channel_count,
            transcendentals=0,
        ),
    )(weight_re, weight_im, spectra)


def cross_kernel(left_ref, right_ref, out_ref):
    spectra_count = left_ref.shape[1]
    left_rows = left_ref.shape[3]
    right_rows, lanes = right_ref.shape[3:]
    step = 16
    for lane in range(0, lanes, 128):
        cols = pl.ds(lane, 128)
        for row in range(0, right_rows, step):
            at = pl.ds(row, step)
            right = [
                (right_ref[0, s, 0, at, cols], right_ref[0, s, 1, at, cols])
                for s in range(spectra_count)
            ]

            def eight_rows(group, carry):
                first = pl.multiple_of(group * 8, 8)
                left = [
                    (left_ref[0, s, 0, pl.ds(first, 8), cols], left_ref[0, s, 1, pl.ds(first, 8), cols])
                    for s in range(spectra_count)
                ]
                for i in range(8):
                    re = jnp.zeros((step, 128), jnp.float32)
                    im = jnp.zeros((step, 128), jnp.float32)
                    for s in range(spectra_count):
                        l_re, l_im = left[s][0][i : i + 1], left[s][1][i : i + 1]
                        r_re, r_im = right[s]
                        re = re + (l_re * r_re + l_im * r_im)
                        im = im + (l_im * r_re - l_re * r_im)
                    out_ref[first + i, 0, 0, at, cols] = re.astype(out_ref.dtype)
                    out_ref[first + i, 0, 1, at, cols] = im.astype(out_ref.dtype)
                return carry

            lax.fori_loop(0, left_rows // 8, eight_rows, 0)


def cross_products(left, right):
    pairs, spectra_count, _, left_rows, channel_count = left.shape
    right_rows = right.shape[3]
    block = min(256, channel_count)
    return pl.pallas_call(
        cross_kernel,
        grid=(pairs, channel_count // block),
        in_specs=[
            pl.BlockSpec(
                (1, spectra_count, 2, left_rows, block), lambda b, k: (b, 0, 0, 0, k)
            ),
            pl.BlockSpec(
                (1, spectra_count, 2, right_rows, block), lambda b, k: (b, 0, 0, 0, k)
            ),
        ],
        out_specs=pl.BlockSpec((left_rows, 1, 2, right_rows, block), lambda b, k: (0, b, 0, 0, k)),
        out_shape=jax.ShapeDtypeStruct(
            (left_rows, pairs, 2, right_rows, channel_count), jnp.bfloat16
        ),
        compiler_params=pltpu.CompilerParams(vmem_limit_bytes=40 * 2**20),
    )(left, right)


def on_device(voltages, pfb_coeffs, beam_delays, slot_of_input, block_list):
    tap_count = pfb_coeffs.shape[0]
    rows_dev = voltages.shape[0]
    frame_len = pfb_coeffs.shape[1]
    spectra_dev = voltages.shape[1] // frame_len
    shards = lax.axis_size("ct") * lax.axis_size("pol")
    channel_count = NCH // shards
    inputs_all = shards * rows_dev
    half_len = FFT_B // 2
    first_table, twist_re, twist_im, second = make_tables(FFT_A, FFT_B)
    second_split = second.reshape(2, 2, shards, half_len // shards, FFT_B)

    first_channel = (
        lax.axis_index("ct") * lax.axis_size("pol") + lax.axis_index("pol")
    ) * channel_count
    channels = (first_channel + jnp.arange(channel_count, dtype=jnp.int32)).astype(jnp.float32)
    ratio = NCH / (NCH + channels)
    delays_slot = jnp.zeros_like(beam_delays).at[:, slot_of_input].set(beam_delays)
    phases = delays_slot[:, :, None] * ratio[None, None, :] * (2.0 * math.pi)
    norm_scale = inputs_all ** (-0.5)
    weight_shape = (beam_delays.shape[0], shards, rows_dev, channel_count)
    weight_re = (jnp.cos(phases) * norm_scale).astype(jnp.bfloat16).reshape(weight_shape)
    weight_im = (-jnp.sin(phases) * norm_scale).astype(jnp.bfloat16).reshape(weight_shape)

    members = jnp.arange(BLK, dtype=jnp.int32)
    needed = slot_of_input[block_list.T[:, :, None] * BLK + members].reshape(-1)
    pick = (needed[:, None] == jnp.arange(inputs_all, dtype=jnp.int32)[None, :]).astype(
        jnp.bfloat16
    )

    frames = {
        index: voltages[:, index * frame_len : (index + 1) * frame_len]
        for index in range(spectra_dev)
    }

    def channelize(taps):
        filtered = jnp.zeros((rows_dev, frame_len), jnp.float32)
        for tap_index in range(tap_count):
            filtered = filtered + pfb_coeffs[tap_index][None, :] * taps[
                tap_index
            ].astype(jnp.float32)
        shaped = filtered.astype(jnp.bfloat16).reshape(rows_dev, FFT_A, FFT_B)
        section_one = jnp.einsum(
            "ckn,rnm->rckm", first_table, shaped, preferred_element_type=jnp.float32
        )
        real_part = section_one[:, 0] * twist_re - section_one[:, 1] * twist_im
        imag_part = section_one[:, 0] * twist_im + section_one[:, 1] * twist_re
        twisted = jnp.stack([real_part, imag_part], 1).astype(jnp.bfloat16)
        outgoing = jnp.einsum(
            "ocdqm,rckm->dorqk", second_split, twisted, preferred_element_type=jnp.float32
        ).astype(jnp.bfloat16)
        return outgoing.reshape(shards, 2, rows_dev, channel_count)

    last = None
    weights = [weight_re, weight_im]
    for back in range(1, tap_count):
        own = frames[spectra_dev - back]
        if last is not None:
            own, last = lax.optimization_barrier((own, last))
        arriving = shifted(own, "tm", 1)
        if back <= 2:
            arriving, weights[back - 1] = lax.optimization_barrier((arriving, weights[back - 1]))
        last = frames[-back] = arriving

    beam_parts = [None] * spectra_dev
    gathered = [None] * spectra_dev
    outgoing = None
    for s in reversed(range(spectra_dev)):
        taps = [frames[s + tap_index - (tap_count - 1)] for tap_index in range(tap_count)]
        if outgoing is not None:
            taps, _ = lax.optimization_barrier((taps, outgoing))
        outgoing = channelize(taps)
        arrived = lax.all_to_all(outgoing, ("ct", "pol"), split_axis=0, concat_axis=0, tiled=True)
        chosen = jnp.stack(
            [
                jnp.dot(
                    pick,
                    arrived[:, part].reshape(inputs_all, channel_count),
                    preferred_element_type=jnp.float32,
                ).astype(jnp.bfloat16)
                for part in range(2)
            ]
        )
        gathered[s] = lax.all_gather(chosen, "tm", axis=0)
        beam_parts[s] = form_beams(weights[0], weights[1], arrived)

    beams = (
        jnp.stack(beam_parts)
        .reshape(spectra_dev, -1, 2, channel_count)
        .transpose(1, 0, 2, 3)
        .astype(jnp.bfloat16)
    )

    pairs = block_list.shape[0]
    steps = lax.axis_size("tm")
    rows = jnp.stack(gathered, 1).reshape(
        steps * spectra_dev, 2, 2, pairs, BLK, channel_count
    )
    own_rows = BLK // steps
    left = lax.dynamic_slice_in_dim(rows[:, :, 0], lax.axis_index("tm") * own_rows, own_rows, 3)
    left = left.transpose(2, 0, 1, 3, 4).astype(jnp.float32)
    right = rows[:, :, 1].transpose(2, 0, 1, 3, 4).astype(jnp.float32)
    return (cross_products(left, right), beams)


def solution(mesh):
    return jax.shard_map(
        on_device,
        mesh=mesh,
        in_specs=(P(("grp", "ct", "pol"), "tm"), P(), P(), P(), P()),
        out_specs=(P("tm", "grp", None, None, ("ct", "pol")), P("grp", "tm", None, ("ct", "pol"))),
        check_vma=False,
    )
```

```python
import math

import jax
import jax.numpy as jnp
from jax import lax
from jax.experimental import pallas as pl
from jax.experimental.pallas import tpu as pltpu
from jax.sharding import PartitionSpec as P

NCH = 8192
BLK = 64
FFT_A = 128
FFT_B = 128


def shifted(block, axis, distance):
    devices = range(lax.axis_size(axis))
    route = [(i - distance, i) for i in devices if i - distance in devices]
    return lax.ppermute(block, axis, route)


def make_tables(first_len, second_len):
    frame_len = first_len * second_len
    half_len = second_len // 2
    rows_a = jnp.arange(first_len, dtype=jnp.int32)
    phase_a = (rows_a[:, None] * rows_a[None, :] % first_len).astype(jnp.float32) * (
        2.0 * math.pi / first_len
    )
    first_table = (jnp.stack([jnp.cos(phase_a), -jnp.sin(phase_a)]) * first_len ** (-0.5)).astype(
        jnp.bfloat16
    )
    cols_b = jnp.arange(second_len, dtype=jnp.int32)
    phase_t = (rows_a[:, None] * cols_b[None, :] % frame_len).astype(jnp.float32) * (
        2.0 * math.pi / frame_len
    )
    twist_re = jnp.cos(phase_t)
    twist_im = -jnp.sin(phase_t)
    rows_h = jnp.arange(half_len, dtype=jnp.int32)
    phase_b = (rows_h[:, None] * cols_b[None, :] % second_len).astype(jnp.float32) * (
        2.0 * math.pi / second_len
    )
    cos_b = jnp.cos(phase_b) * second_len ** (-0.5)
    sin_b = -jnp.sin(phase_b) * second_len ** (-0.5)
    second = jnp.stack([jnp.stack([cos_b, -sin_b]), jnp.stack([sin_b, cos_b])]).astype(jnp.bfloat16)
    return (first_table, twist_re, twist_im, second)


def beam_kernel(weight_re_ref, weight_im_ref, spectra_ref, out_ref):
    beam_count, shards, rows, lanes = weight_re_ref.shape
    step = 16
    for lane in range(0, lanes, 128):
        cols = pl.ds(lane, 128)

        def add(t, totals):
            d = t // (rows // step)
            at = pl.ds(pl.multiple_of(t % (rows // step) * step, step), step)
            re = spectra_ref[d, 0, at, cols].astype(jnp.float32)
            im = spectra_ref[d, 1, at, cols].astype(jnp.float32)
            sums = []
            for e in range(beam_count):
                w_re = weight_re_ref[e, d, at, cols].astype(jnp.float32)
                w_im = weight_im_ref[e, d, at, cols].astype(jnp.float32)
                sums.append(totals[2 * e] + (w_re * re - w_im * im))
                sums.append(totals[2 * e + 1] + (w_im * re + w_re * im))
            return tuple(sums)

        zeros = tuple(jnp.zeros((step, 128), jnp.float32) for _ in range(2 * beam_count))
        totals = lax.fori_loop(0, shards * rows // step, add, zeros)
        out_ref[:, cols] = jnp.concatenate(
            [jnp.sum(total, axis=0, keepdims=True) for total in totals], axis=0
        )


def form_beams(weight_re, weight_im, spectra):
    beam_count, shards, rows, channel_count = weight_re.shape
    block = min(256, channel_count)
    weight_spec = pl.BlockSpec((beam_count, shards, rows, block), lambda k: (0, 0, 0, k))
    return pl.pallas_call(
        beam_kernel,
        grid=(channel_count // block,),
        in_specs=[
            weight_spec,
            weight_spec,
            pl.BlockSpec((shards, 2, rows, block), lambda k: (0, 0, 0, k)),
        ],
        out_specs=pl.BlockSpec((2 * beam_count, block), lambda k: (0, k)),
        out_shape=jax.ShapeDtypeStruct((2 * beam_count, channel_count), jnp.float32),
        compiler_params=pltpu.CompilerParams(vmem_limit_bytes=40 * 2**20),
        cost_estimate=pl.CostEstimate(
            flops=16 * beam_count * shards * rows * channel_count,
            bytes_accessed=4 * (beam_count + 1) * shards * rows * channel_count,
            transcendentals=0,
        ),
    )(weight_re, weight_im, spectra)


def cross_kernel(left_ref, right_ref, out_ref):
    spectra_count = left_ref.shape[1]
    left_rows = left_ref.shape[3]
    right_rows, lanes = right_ref.shape[3:]
    step = 16
    for lane in range(0, lanes, 128):
        cols = pl.ds(lane, 128)
        for row in range(0, right_rows, step):
            at = pl.ds(row, step)
            right = [
                (right_ref[0, s, 0, at, cols], right_ref[0, s, 1, at, cols])
                for s in range(spectra_count)
            ]

            def eight_rows(group, carry):
                first = pl.multiple_of(group * 8, 8)
                left = [
                    (left_ref[0, s, 0, pl.ds(first, 8), cols], left_ref[0, s, 1, pl.ds(first, 8), cols])
                    for s in range(spectra_count)
                ]
                for i in range(8):
                    re = jnp.zeros((step, 128), jnp.float32)
                    im = jnp.zeros((step, 128), jnp.float32)
                    for s in range(spectra_count):
                        l_re, l_im = left[s][0][i : i + 1], left[s][1][i : i + 1]
                        r_re, r_im = right[s]
                        re = re + (l_re * r_re + l_im * r_im)
                        im = im + (l_im * r_re - l_re * r_im)
                    out_ref[first + i, 0, 0, at, cols] = re.astype(out_ref.dtype)
                    out_ref[first + i, 0, 1, at, cols] = im.astype(out_ref.dtype)
                return carry

            lax.fori_loop(0, left_rows // 8, eight_rows, 0)


def cross_products(left, right):
    pairs, spectra_count, _, left_rows, channel_count = left.shape
    right_rows = right.shape[3]
    block = min(256, channel_count)
    return pl.pallas_call(
        cross_kernel,
        grid=(pairs, channel_count // block),
        in_specs=[
            pl.BlockSpec(
                (1, spectra_count, 2, left_rows, block), lambda b, k: (b, 0, 0, 0, k)
            ),
            pl.BlockSpec(
                (1, spectra_count, 2, right_rows, block), lambda b, k: (b, 0, 0, 0, k)
            ),
        ],
        out_specs=pl.BlockSpec((left_rows, 1, 2, right_rows, block), lambda b, k: (0, b, 0, 0, k)),
        out_shape=jax.ShapeDtypeStruct(
            (left_rows, pairs, 2, right_rows, channel_count), jnp.bfloat16
        ),
        compiler_params=pltpu.CompilerParams(vmem_limit_bytes=40 * 2**20),
    )(left, right)


def on_device(voltages, pfb_coeffs, beam_delays, slot_of_input, block_list):
    tap_count = pfb_coeffs.shape[0]
    rows_dev = voltages.shape[0]
    frame_len = pfb_coeffs.shape[1]
    spectra_dev = voltages.shape[1] // frame_len
    shards = lax.axis_size("ct") * lax.axis_size("pol")
    channel_count = NCH // shards
    inputs_all = shards * rows_dev
    half_len = FFT_B // 2
    first_table, twist_re, twist_im, second = make_tables(FFT_A, FFT_B)
    second_split = second.reshape(2, 2, shards, half_len // shards, FFT_B)

    first_channel = (
        lax.axis_index("ct") * lax.axis_size("pol") + lax.axis_index("pol")
    ) * channel_count
    channels = (first_channel + jnp.arange(channel_count, dtype=jnp.int32)).astype(jnp.float32)
    ratio = NCH / (NCH + channels)
    delays_slot = jnp.zeros_like(beam_delays).at[:, slot_of_input].set(beam_delays)
    phases = delays_slot[:, :, None] * ratio[None, None, :] * (2.0 * math.pi)
    norm_scale = inputs_all ** (-0.5)
    weight_shape = (beam_delays.shape[0], shards, rows_dev, channel_count)
    weight_re = (jnp.cos(phases) * norm_scale).astype(jnp.bfloat16).reshape(weight_shape)
    weight_im = (-jnp.sin(phases) * norm_scale).astype(jnp.bfloat16).reshape(weight_shape)

    members = jnp.arange(BLK, dtype=jnp.int32)
    needed = slot_of_input[block_list.T[:, :, None] * BLK + members].reshape(-1)
    pick = (needed[:, None] == jnp.arange(inputs_all, dtype=jnp.int32)[None, :]).astype(
        jnp.bfloat16
    )

    frames = {
        index: voltages[:, index * frame_len : (index + 1) * frame_len]
        for index in range(spectra_dev)
    }

    def channelize(taps):
        filtered = jnp.zeros((rows_dev, frame_len), jnp.float32)
        for tap_index in range(tap_count):
            filtered = filtered + pfb_coeffs[tap_index][None, :] * taps[
                tap_index
            ].astype(jnp.float32)
        shaped = filtered.astype(jnp.bfloat16).reshape(rows_dev, FFT_A, FFT_B)
        section_one = jnp.einsum(
            "ckn,rnm->rckm", first_table, shaped, preferred_element_type=jnp.float32
        )
        real_part = section_one[:, 0] * twist_re - section_one[:, 1] * twist_im
        imag_part = section_one[:, 0] * twist_im + section_one[:, 1] * twist_re
        twisted = jnp.stack([real_part, imag_part], 1).astype(jnp.bfloat16)
        outgoing = jnp.einsum(
            "ocdqm,rckm->dorqk", second_split, twisted, preferred_element_type=jnp.float32
        ).astype(jnp.bfloat16)
        return outgoing.reshape(shards, 2, rows_dev, channel_count)

    last = None
    weights = [weight_re, weight_im]
    for back in range(1, tap_count):
        own = frames[spectra_dev - back]
        if last is not None:
            own, last = lax.optimization_barrier((own, last))
        arriving = shifted(own, "tm", 1)
        if back <= 2:
            arriving, weights[back - 1] = lax.optimization_barrier((arriving, weights[back - 1]))
        last = frames[-back] = arriving

    beam_parts = [None] * spectra_dev
    gathered = [None] * spectra_dev
    outgoing = None
    for s in reversed(range(spectra_dev)):
        taps = [frames[s + tap_index - (tap_count - 1)] for tap_index in range(tap_count)]
        if outgoing is not None:
            taps, _ = lax.optimization_barrier((taps, outgoing))
        outgoing = channelize(taps)
        arrived = lax.all_to_all(outgoing, ("ct", "pol"), split_axis=0, concat_axis=0, tiled=True)
        if s + 1 < spectra_dev:
            arrived, beam_parts[s + 1] = lax.optimization_barrier((arrived, beam_parts[s + 1]))
        chosen = jnp.stack(
            [
                jnp.dot(
                    pick,
                    arrived[:, part].reshape(inputs_all, channel_count),
                    preferred_element_type=jnp.float32,
                ).astype(jnp.bfloat16)
                for part in range(2)
            ]
        )
        gathered[s] = lax.all_gather(chosen, "tm", axis=0)
        beam_parts[s] = form_beams(weights[0], weights[1], arrived)

    beams = (
        jnp.stack(beam_parts)
        .reshape(spectra_dev, -1, 2, channel_count)
        .transpose(1, 0, 2, 3)
        .astype(jnp.bfloat16)
    )

    pairs = block_list.shape[0]
    steps = lax.axis_size("tm")
    rows = jnp.stack(gathered, 1).reshape(
        steps * spectra_dev, 2, 2, pairs, BLK, channel_count
    )
    own_rows = BLK // steps
    left = lax.dynamic_slice_in_dim(rows[:, :, 0], lax.axis_index("tm") * own_rows, own_rows, 3)
    left = left.transpose(2, 0, 1, 3, 4).astype(jnp.float32)
    right = rows[:, :, 1].transpose(2, 0, 1, 3, 4).astype(jnp.float32)
    return (cross_products(left, right), beams)


def solution(mesh):
    return jax.shard_map(
        on_device,
        mesh=mesh,
        in_specs=(P(("grp", "ct", "pol"), "tm"), P(), P(), P(), P()),
        out_specs=(P("tm", "grp", None, None, ("ct", "pol")), P("grp", "tm", None, ("ct", "pol"))),
        check_vma=False,
    )
```
